32 devices in a mesh: thinker: 4 (over z), seq: 8 (over y, x, core).
Axes of the slice: x: 2, y: 2, z: 4, core: 2. Of those that a mesh axis runs over, the one named last changes fastest.
Arguments:
- queries: bfloat16 [4, 1024, 2048], P('thinker', 'seq'), may hold values from -6 to 6
- keys: bfloat16 [4, 1024, 512], P('thinker', 'seq'), may hold values from -6 to 6
- values: bfloat16 [4, 1024, 512], P('thinker', 'seq'), may hold values from -6 to 6
- forward_out: bfloat16 [4, 1024, 2048], P('thinker', 'seq'), may hold values from -2 to 2
- logsumexp: float32 [4, 16, 1024], P('thinker', None, 'seq'), may hold values from -1 to 16, as said below
- upstream: bfloat16 [128, 32, 2048], P(None, ('thinker', 'seq')), may hold values from -6 to 6
- lengths: int32 [4], replicated, may hold values from 128 to 1024, as said below
- sibling_mask: int32 [4, 3, 8], P('thinker', None, 'seq'), may hold values from 0 to 1, as said below
Outputs:
- query_grad: bfloat16 [4, 1024, 2048], P('thinker', 'seq')
- key_grad: bfloat16 [4, 1024, 512], P('thinker', 'seq')
- value_grad: bfloat16 [4, 1024, 512], P('thinker', 'seq')
The draws below stay inside these ranges and needn't reach their ends.
Inputs may be any that keep to these rules, and one draw needn't show every extreme that they name: lengths[t] valid positions stand at the start of thinker t's trace; two thinkers have exactly 1024, one exactly 128. sibling_mask[t, r, b] = 1 where query block b of thinker t reads the recent tokens of thinker (t + r + 1) % 4; the two thinkers of length 1024 read each other in the blocks of the last 128 positions. `logsumexp`: rows of positions past a trace's length carry arbitrary values.
All inputs are finite; a program needn't handle non-finite values.
Results may differ from the reference program's by a relative error of at most 0.014.
Values may be sent and summed in bfloat16 or wider, within the bound.
A program may use at most 128 MiB of HBM per device.

```python
import jax
import jax.numpy as jnp
from jax import lax

TOK_DEV = 128
HEADS = 16
KV_HEADS = 4
HD = 128
BLOCK = 128
THINKERS = 4
SHARDS = 8
LENGTH = 1024
GROUP = 4
QW = 2048
KW = 512
N_SEQ = 8


def shared_draw(key):
    length = TOK_DEV * N_SEQ
    blocks = length // BLOCK
    order = jax.random.permutation(jax.random.fold_in(key, 101), THINKERS)
    spans = jax.random.randint(jax.random.fold_in(key, 102), (THINKERS,), length // 8, length + 1)
    spans = spans.at[order[0]].set(length)
    spans = spans.at[order[1]].set(length)
    spans = spans.at[order[2]].set(length // 8)
    visible = jax.random.randint(jax.random.fold_in(key, 103), (THINKERS, THINKERS - 1, blocks), 0, 2)
    block_ids = jnp.arange(blocks, dtype=jnp.int32)
    last_blocks = block_ids >= blocks - TOK_DEV // BLOCK
    first_reads = (order[1] - order[0] - 1) % THINKERS
    second_reads = (order[0] - order[1] - 1) % THINKERS
    thinker_ids = jnp.arange(THINKERS, dtype=jnp.int32)[:, None, None]
    offset_ids = jnp.arange(THINKERS - 1, dtype=jnp.int32)[None, :, None]
    forced = (thinker_ids == order[0]) & (offset_ids == first_reads) | (thinker_ids == order[1]) & (offset_ids == second_reads)
    forced = forced & last_blocks[None, None, :]
    visible = jnp.where(forced, 1, visible)
    return (spans.astype(jnp.int32), visible.astype(jnp.int32))


def draw_lengths(key, part):
    return shared_draw(key)[0]


def draw_sibling_mask(key, part):
    return shared_draw(key)[1]


def draw_logsumexp(key, part):
    length = TOK_DEV * N_SEQ
    spans, visible = shared_draw(key)
    positions = jnp.arange(length, dtype=jnp.int32)
    counts = jnp.where(positions[None, :] < spans[:, None], positions[None, :] + 1, 0)
    block_ids = positions // BLOCK
    lowest = jnp.maximum(positions - TOK_DEV + 1, 0)
    thinker_ids = jnp.arange(THINKERS, dtype=jnp.int32)
    for offset in range(1, THINKERS):
        sibling_len = spans[(thinker_ids + offset) % THINKERS]
        highest = jnp.minimum(positions[None, :], sibling_len[:, None] - 1)
        reach = jnp.maximum(highest - lowest[None, :] + 1, 0)
        counts = counts + visible[:, offset - 1][:, block_ids] * reach
    base = 0.5 * jnp.log(jnp.maximum(counts, 1).astype(jnp.float32)) + 0.5
    noise = jax.random.uniform(jax.random.fold_in(key, 104), (THINKERS, HEADS, length), jnp.float32, -0.5, 0.5)
    return base[:, None, :] + noise


def block_levels(rng, shape, cuts, smallest, top_value):
    def one(axis_at, blocks):
        draws = jax.random.uniform(jax.random.fold_in(jax.random.fold_in(rng, 6), axis_at), (blocks,), jnp.float32, smallest / len(cuts), top_value / len(cuts))
        return jnp.repeat(jnp.exp(draws), shape[axis_at] // blocks).reshape((-1,) + (1,) * (len(shape) - axis_at - 1))

    level = one(*cuts[0])
    for cut in cuts[1:]:
        level = level * one(*cut)
    return level


def scatter_about(stream_key, extent, width, most, pieces=(), kind=jnp.bfloat16):
    array = jax.random.normal(stream_key, extent, jnp.float32) * width
    if len(pieces) > 0:
        array = block_levels(stream_key, extent, pieces, -0.22, 0.18) * array
    return jnp.clip(array, min=-most, max=most).astype(kind)


def setup_inputs(seed: int = 0) -> dict:
    streams_of = jax.random.split(jax.random.key(seed), 9)
    return {
        "queries": scatter_about(streams_of[0], (THINKERS, LENGTH, QW), 1.0, 6.0, ((0, 4), (1, 8))),
        "keys": scatter_about(streams_of[1], (THINKERS, LENGTH, KW), 1.0, 6.0, ((0, 4), (1, 8))),
        "values": scatter_about(streams_of[2], (THINKERS, LENGTH, KW), 1.0, 6.0, ((0, 4), (1, 8))),
        "forward_out": scatter_about(streams_of[3], (THINKERS, LENGTH, QW), 0.3, 2.0, ((0, 4), (1, 8))),
        "logsumexp": draw_logsumexp(jax.random.fold_in(streams_of[8], 71), 0),
        "upstream": scatter_about(streams_of[5], (TOK_DEV, THINKERS * SHARDS, QW), 1.0, 6.0, ((1, 32),)),
        "lengths": draw_lengths(jax.random.fold_in(streams_of[8], 71), 0),
        "sibling_mask": draw_sibling_mask(jax.random.fold_in(streams_of[8], 71), 0),
    }


def pair_grads(query_heads, upstream_heads, lse_heads, delta_heads, key_rows, value_rows, allowed, factor):
    count = key_rows.shape[0]
    kv_heads = query_heads.shape[1]
    head_dim = query_heads.shape[3]
    query_wide = query_heads.astype(jnp.float32)
    upstream_wide = upstream_heads.astype(jnp.float32)
    key_heads = key_rows.reshape(count, kv_heads, head_dim).astype(jnp.float32)
    value_heads = value_rows.reshape(count, kv_heads, head_dim).astype(jnp.float32)
    scores = jnp.einsum("ikgd,jkd->kgij", query_wide, key_heads) * factor
    probs = jnp.where(allowed, jnp.exp(scores - lse_heads[..., None]), 0.0)
    dprobs = jnp.einsum("ikgd,jkd->kgij", upstream_wide, value_heads)
    dscores = probs * (dprobs - delta_heads[..., None])
    probs_low = lax.optimization_barrier(probs.astype(jnp.bfloat16)).astype(jnp.float32)
    dscores_low = lax.optimization_barrier(dscores.astype(jnp.bfloat16)).astype(jnp.float32)
    value_part = jnp.einsum("kgij,ikgd->jkd", probs_low, upstream_wide)
    key_part = jnp.einsum("kgij,ikgd->jkd", dscores_low, query_wide) * factor
    query_part = jnp.einsum("kgij,jkd->ikgd", dscores_low, key_heads) * factor
    rows = query_heads.shape[0]
    return query_part.reshape(rows, -1), key_part.reshape(count, -1), value_part.reshape(count, -1)


def round_low(term):
    return lax.optimization_barrier(term.astype(jnp.bfloat16)).astype(jnp.float32)


def reference(queries, keys, values, forward_out, logsumexp, upstream, lengths, sibling_mask):
    length = TOK_DEV * N_SEQ
    factor = HD ** -0.5
    kwidth = KV_HEADS * HD
    grad_out = upstream.reshape(THINKERS, length, HEADS * HD)
    delta = jnp.sum((grad_out.astype(jnp.float32) * forward_out.astype(jnp.float32)).reshape(THINKERS, length, KV_HEADS, GROUP, HD), axis=-1)
    positions = jnp.arange(length, dtype=jnp.int32)
    local = jnp.arange(TOK_DEV, dtype=jnp.int32)
    window = jnp.arange(2 * TOK_DEV, dtype=jnp.int32)
    key_grad = jnp.zeros((THINKERS, length, kwidth), jnp.float32)
    value_grad = jnp.zeros((THINKERS, length, kwidth), jnp.float32)
    padded_keys = [jnp.concatenate([jnp.zeros((TOK_DEV, kwidth), keys.dtype), keys[u]], axis=0) for u in range(THINKERS)]
    padded_values = [jnp.concatenate([jnp.zeros((TOK_DEV, kwidth), values.dtype), values[u]], axis=0) for u in range(THINKERS)]
    query_list = []
    for thinker in range(THINKERS):
        own_length = lengths[thinker]

        def shard_step(carry, shard):
            key_acc, value_acc = carry
            start = (shard * TOK_DEV).astype(jnp.int32)
            query_pos = start + local
            live = query_pos < own_length
            query_heads = lax.dynamic_slice_in_dim(queries[thinker], start, TOK_DEV, 0).reshape(TOK_DEV, KV_HEADS, GROUP, HD)
            upstream_heads = lax.dynamic_slice_in_dim(grad_out[thinker], start, TOK_DEV, 0).reshape(TOK_DEV, KV_HEADS, GROUP, HD)
            lse_heads = lax.dynamic_slice_in_dim(logsumexp[thinker], start, TOK_DEV, 1).reshape(KV_HEADS, GROUP, TOK_DEV)
            delta_heads = jnp.transpose(lax.dynamic_slice_in_dim(delta[thinker], start, TOK_DEV, 0), (1, 2, 0))
            allowed = (positions[None, :] <= query_pos[:, None]) & live[:, None] & (positions[None, :] < own_length)
            query_part, key_part, value_part = pair_grads(query_heads, upstream_heads, lse_heads, delta_heads, keys[thinker], values[thinker], allowed, factor)
            block_ids = query_pos // BLOCK
            key_pos = start - TOK_DEV + window
            near = (key_pos[None, :] <= query_pos[:, None]) & (key_pos[None, :] > query_pos[:, None] - TOK_DEV) & (key_pos[None, :] >= 0) & live[:, None]
            sibling_keys = []
            sibling_values = []
            for offset in range(1, THINKERS):
                sibling = (thinker + offset) % THINKERS
                visible = sibling_mask[thinker, offset - 1][block_ids] == 1
                allowed_sibling = near & visible[:, None] & (key_pos[None, :] < lengths[sibling])
                key_rows = lax.dynamic_slice_in_dim(padded_keys[sibling], start, 2 * TOK_DEV, 0)
                value_rows = lax.dynamic_slice_in_dim(padded_values[sibling], start, 2 * TOK_DEV, 0)
                extra_query, extra_key, extra_value = pair_grads(query_heads, upstream_heads, lse_heads, delta_heads, key_rows, value_rows, allowed_sibling, factor)
                query_part = query_part + extra_query
                sibling_keys.append(extra_key)
                sibling_values.append(extra_value)
            new_carry = (key_acc + round_low(key_part), value_acc + round_low(value_part))
            return new_carry, (query_part, jnp.stack(sibling_keys), jnp.stack(sibling_values))

        empty = jnp.zeros((length, kwidth), jnp.float32)
        (own_key, own_value), (query_parts, sib_key, sib_value) = lax.scan(shard_step, (empty, empty), jnp.arange(N_SEQ, dtype=jnp.int32))
        query_list.append(query_parts.reshape(length, HEADS * HD))
        key_grad = key_grad.at[thinker].add(own_key)
        value_grad = value_grad.at[thinker].add(own_value)
        tail = jnp.zeros((TOK_DEV, kwidth), jnp.float32)
        for offset in range(1, THINKERS):
            sibling = (thinker + offset) % THINKERS
            part_key = sib_key[:, offset - 1]
            part_value = sib_value[:, offset - 1]
            upper_key = part_key[:, TOK_DEV:].reshape(length, kwidth)
            lower_key = part_key[:, :TOK_DEV].reshape(length, kwidth)
            upper_value = part_value[:, TOK_DEV:].reshape(length, kwidth)
            lower_value = part_value[:, :TOK_DEV].reshape(length, kwidth)
            key_grad = key_grad.at[sibling].add(upper_key + jnp.concatenate([lower_key[TOK_DEV:], tail], axis=0))
            value_grad = value_grad.at[sibling].add(upper_value + jnp.concatenate([lower_value[TOK_DEV:], tail], axis=0))
    query_grad = jnp.stack(query_list).astype(jnp.bfloat16)
    return query_grad, key_grad.astype(jnp.bfloat16), value_grad.astype(jnp.bfloat16)
```

```python
import functools
import math

import jax
import jax.numpy as jnp
from jax import lax
from jax.experimental import pallas as pl
from jax.experimental.pallas import tpu as pltpu
from jax.sharding import PartitionSpec as P

BLOCK = 128
MESH = pl.DeviceIdType.MESH
F32 = jnp.float32
BF16 = jnp.bfloat16
FAR = 1e30


def dot_tt(a, b):
    return lax.dot_general(a, b, (((1,), (1,)), ((), ())), preferred_element_type=F32)


def dot_nn(a, b):
    return lax.dot_general(a, b, (((1,), (0,)), ((), ())), preferred_element_type=F32)


def dot_t(a, b):
    return lax.dot_general(a, b, (((0,), (0,)), ((), ())), preferred_element_type=F32)


def body(
    T, S, G, KV, HD,
    lengths, mask, q_ref, k_ref, v_ref, o_ref, lse_ref, up_ref,
    dq_ref, dk_ref, dv_ref,
    rows_in, kvall, sibc, sibp, gpart, gown, gsp, gspr, gsc, gz, gzr,
    qs, dos, lse2, delta, dqa, acc,
    up_send, up_recv, kv_send, kv_recv, z_send, z_recv, h_send, h_recv,
    g_send, g_recv, b_send, b_recv, y_send, y_recv,
):
    N = T * S
    ROWS = 128
    W = up_ref.shape[1]
    C = (KV * G * HD) // W
    shift = int(math.log2(N))
    GQ = G * ROWS
    factor = HD ** (-0.5)
    log2e = math.log2(math.e)
    t = lax.axis_index("thinker")
    s = lax.axis_index("seq")
    me = t * S + s

    def place(d):
        return (d // S, d % S)

    barrier = pltpu.get_barrier_semaphore()

    def greet(i, c):
        pl.semaphore_signal(
            barrier, inc=1, device_id=place(lax.rem(me + i, N)), device_id_type=MESH
        )
        return c

    lax.fori_loop(1, N, greet, 0)

    for g in range(KV):
        kvall[s, g] = k_ref[:, g * HD:(g + 1) * HD]
        kvall[s, KV + g] = v_ref[:, g * HD:(g + 1) * HD]

    pl.semaphore_wait(barrier, N - 1)

    def remote(src, dst, ss, rs, where):
        return pltpu.make_async_remote_copy(
            src_ref=src, dst_ref=dst, send_sem=ss, recv_sem=rs,
            device_id=where, device_id_type=MESH,
        )

    def send_up(i, c):
        d = lax.rem(me + i, N)
        remote(
            up_ref.at[pl.ds(pl.multiple_of(d * 16, 16), 16)],
            rows_in.at[pl.ds(pl.multiple_of(me * 16, 16), 16)],
            up_send, up_recv, place(d),
        ).start()
        return c

    lax.fori_loop(1, N, send_up, 0)

    def z_copy(o):
        return remote(
            kvall.at[s], sibc.at[o - 1], z_send.at[o - 1], z_recv.at[o - 1],
            (lax.rem(t + T - o, T), s),
        )

    for o in range(1, T):
        z_copy(o).start()

    def kv_copy(d):
        return remote(kvall.at[s], kvall.at[s], kv_send.at[d], kv_recv.at[s], (t, d))

    def kv_start(d, c):
        kv_copy(d).start()
        return c

    lax.fori_loop(s + 1, S, kv_start, 0)

    rows_in[pl.ds(pl.multiple_of(me * 16, 16), 16), :] = up_ref[
        pl.ds(pl.multiple_of(me * 16, 16), 16), :
    ]
    mine = lengths[t]
    first = s * ROWS
    lane = lax.broadcasted_iota(jnp.int32, (1, GQ), 1) & (ROWS - 1)
    live = (first + lane) < mine
    for g in range(KV):
        qs[g] = jnp.concatenate(
            [q_ref[:, (g * G + i) * HD:(g * G + i + 1) * HD] for i in range(G)], axis=0
        )
        row = jnp.concatenate([lse_ref[g * G + i:g * G + i + 1, :] for i in range(G)], axis=1)
        lse2[g] = jnp.where(live, row * log2e, FAR)
    dqa[...] = jnp.zeros_like(dqa)

    @pl.when(s == 0)
    def _():
        sibp[...] = jnp.zeros_like(sibp)

    whole = rows_in.at[pl.ds(0, (N - 1) * 16)]
    pltpu.make_async_copy(whole, whole, up_recv).wait()
    pos = lax.broadcasted_iota(jnp.int32, (ROWS, N * 16), 0)
    col = lax.broadcasted_iota(jnp.int32, (ROWS, N * 16), 1)
    base = (pos & (N - 1)) * 16 + lax.shift_right_logical(pos, shift) * C
    arrived = rows_in[...]
    per = W // HD
    for c in range(C):
        pick = jnp.where(col == base + c, 1.0, 0.0).astype(BF16)
        part = dot_nn(pick, arrived).astype(BF16)
        for i in range(per):
            h = c * per + i
            dos[h // G, (h % G) * ROWS:(h % G + 1) * ROWS, :] = part[:, i * HD:(i + 1) * HD]
    ones = jnp.ones((8, HD), BF16)
    for g in range(KV):
        og = jnp.concatenate(
            [o_ref[:, (g * G + i) * HD:(g * G + i + 1) * HD] for i in range(G)], axis=0
        )
        prod = dos[g].astype(F32) * og.astype(F32)
        high = prod.astype(BF16)
        low = (prod - high.astype(F32)).astype(BF16)
        delta[g] = (dot_tt(ones, high) + dot_tt(ones, low))[0:1, :]

    key_i = lax.broadcasted_iota(jnp.int32, (ROWS, GQ), 0)
    qry_i = lax.broadcasted_iota(jnp.int32, (ROWS, GQ), 1) & (ROWS - 1)
    scale = factor * log2e

    def own(b, diagonal):
        def step(g, c):
            km = kvall[b, g]
            vm = kvall[b, KV + g]
            qg = qs[g]
            dg = dos[g]
            p = jnp.exp2(dot_tt(km, qg) * scale - lse2[g])
            if diagonal:
                p = jnp.where(key_i <= qry_i, p, 0.0)
            ds = p * (dot_tt(vm, dg) - delta[g])
            pb = p.astype(BF16)
            db = ds.astype(BF16)
            dv = dot_nn(pb, dg)
            dk = dot_nn(db, qg) * factor
            if diagonal:
                acc[g] = dk
                acc[KV + g] = dv
            else:
                gpart[b, g] = dk.astype(BF16)
                gpart[b, KV + g] = dv.astype(BF16)
            dqa[g] += dot_t(db, km)
            return c

        lax.fori_loop(0, KV, step, 0)

    own(s, True)

    def shift_copy(o):
        return remote(
            sibc.at[o - 1], sibp.at[o - 1], h_send.at[o - 1], h_recv.at[o - 1],
            (t, lax.rem(s + 1, S)),
        )

    def back_copy(o):
        return remote(
            gsp.at[o - 1], gspr.at[o - 1], b_send.at[o - 1], b_recv.at[o - 1],
            (t, lax.rem(s + S - 1, S)),
        )

    for o in range(1, T):
        z_copy(o).wait_recv()

        @pl.when(s < S - 1)
        def _():
            shift_copy(o).start()

    for o in range(1, T):
        @pl.when(s > 0)
        def _():
            shift_copy(o).wait_recv()

        other = lengths[lax.rem(t + o, T)]
        edge = jnp.where(mask[o - 1] == 1, other - first, -2 * ROWS)

        def step(g, c):
            kc = sibc[o - 1, g]
            vc = sibc[o - 1, KV + g]
            kp = sibp[o - 1, g]
            vp = sibp[o - 1, KV + g]
            qg = qs[g]
            dg = dos[g]
            near = key_i <= qry_i
            place_k = jnp.where(near, key_i, key_i - ROWS)
            keep = (place_k < edge) & (place_k >= -first)
            st = jnp.where(near, dot_tt(kc, qg), dot_tt(kp, qg))
            p = jnp.where(keep, jnp.exp2(st * scale - lse2[g]), 0.0)
            dp = jnp.where(near, dot_tt(vc, dg), dot_tt(vp, dg))
            ds = p * (dp - delta[g])
            pc = jnp.where(near, p, 0.0).astype(BF16)
            pp = jnp.where(near, 0.0, p).astype(BF16)
            dc = jnp.where(near, ds, 0.0).astype(BF16)
            de = jnp.where(near, 0.0, ds).astype(BF16)
            gsc[o - 1, g] = dot_nn(dc, qg) * factor
            gsc[o - 1, KV + g] = dot_nn(pc, dg)
            gsp[o - 1, g] = (dot_nn(de, qg) * factor).astype(BF16)
            gsp[o - 1, KV + g] = dot_nn(pp, dg).astype(BF16)
            dqa[g] += dot_t(dc, kc) + dot_t(de, kp)
            return c

        lax.fori_loop(0, KV, step, 0)

        @pl.when(s > 0)
        def _():
            back_copy(o).start()

    def g_copy(b):
        return remote(gpart.at[b], gown.at[s], g_send.at[b], g_recv.at[s], (t, b))

    def kv_arrival(b):
        return remote(kvall.at[b], kvall.at[b], kv_send.at[b], kv_recv.at[b], (t, b))

    def own_step(b, c):
        kv_arrival(b).wait_recv()
        own(b, False)
        g_copy(b).start()
        return c

    half = s // 2
    lax.fori_loop(0, half, own_step, 0)

    def y_copy(o):
        return remote(
            gz.at[o - 1], gzr.at[o - 1], y_send.at[o - 1], y_recv.at[o - 1],
            (lax.rem(t + o, T), s),
        )

    for o in range(1, T):
        @pl.when(s < S - 1)
        def _():
            back_copy(o).wait_recv()
            gz[o - 1] = (gsc[o - 1] + gspr[o - 1].astype(F32)).astype(BF16)

        @pl.when(s == S - 1)
        def _():
            gz[o - 1] = gsc[o - 1].astype(BF16)

        y_copy(o).start()

    lax.fori_loop(half, s, own_step, 0)

    for g in range(KV):
        for i in range(G):
            h = g * G + i
            dq_ref[:, h * HD:(h + 1) * HD] = (
                dqa[g, i * ROWS:(i + 1) * ROWS, :] * factor
            ).astype(BF16)

    def g_arrival(b, c):
        remote(gpart.at[b], gown.at[b], g_send.at[b], g_recv.at[b], (t, b)).wait_recv()
        acc[...] += gown[b].astype(F32)
        return c

    lax.fori_loop(s + 1, S, g_arrival, 0)
    for o in range(1, T):
        y_copy(o).wait_recv()
        acc[...] += gzr[o - 1].astype(F32)
    for g in range(KV):
        dk_ref[:, g * HD:(g + 1) * HD] = acc[g].astype(BF16)
        dv_ref[:, g * HD:(g + 1) * HD] = acc[KV + g].astype(BF16)

    sent = up_ref.at[pl.ds(0, (N - 1) * 16)]
    pltpu.make_async_copy(sent, sent, up_send).wait()

    def kv_left(d, c):
        kv_copy(d).wait_send()
        return c

    lax.fori_loop(s + 1, S, kv_left, 0)

    def g_left(b, c):
        g_copy(b).wait_send()
        return c

    lax.fori_loop(0, s, g_left, 0)
    for o in range(1, T):
        z_copy(o).wait_send()
        y_copy(o).wait_send()

        @pl.when(s < S - 1)
        def _():
            shift_copy(o).wait_send()

        @pl.when(s > 0)
        def _():
            back_copy(o).wait_send()


def shards(queries, keys, values, forward_out, logsumexp, upstream, lengths, sibling_mask):
    T = lax.axis_size("thinker")
    S = lax.axis_size("seq")
    N = T * S
    rows, qw = queries.shape[1:]
    kw = keys.shape[2]
    heads = logsumexp.shape[1]
    HD = qw // heads
    KV = kw // HD
    G = heads // KV
    width = (rows // N) * qw // 16
    up = upstream.reshape(N * 16, width)
    block = (2 * KV, rows, HD)
    vmem = pl.BlockSpec(memory_space=pltpu.VMEM)
    smem = pl.BlockSpec(memory_space=pltpu.SMEM)
    dma = pltpu.SemaphoreType.DMA
    dq, dk, dv = pl.pallas_call(
        functools.partial(body, T, S, G, KV, HD),
        out_shape=(
            jax.ShapeDtypeStruct((rows, qw), BF16),
            jax.ShapeDtypeStruct((rows, kw), BF16),
            jax.ShapeDtypeStruct((rows, kw), BF16),
        ),
        in_specs=[smem, smem] + [vmem] * 6,
        out_specs=(vmem, vmem, vmem),
        scratch_shapes=[
            pltpu.VMEM((N * 16, width), BF16),
            pltpu.VMEM((S,) + block, BF16),
            pltpu.VMEM((T - 1,) + block, BF16),
            pltpu.VMEM((T - 1,) + block, BF16),
            pltpu.VMEM((S,) + block, BF16),
            pltpu.VMEM((S,) + block, BF16),
            pltpu.VMEM((T - 1,) + block, BF16),
            pltpu.VMEM((T - 1,) + block, BF16),
            pltpu.VMEM((T - 1,) + block, F32),
            pltpu.VMEM((T - 1,) + block, BF16),
            pltpu.VMEM((T - 1,) + block, BF16),
            pltpu.VMEM((KV, G * rows, HD), BF16),
            pltpu.VMEM((KV, G * rows, HD), BF16),
            pltpu.VMEM((KV, 1, G * rows), F32),
            pltpu.VMEM((KV, 1, G * rows), F32),
            pltpu.VMEM((KV, G * rows, HD), F32),
            pltpu.VMEM(block, F32),
            dma, dma, dma((S,)), dma((S,)), dma((T - 1,)), dma((T - 1,)),
            dma((T - 1,)), dma((T - 1,)), dma((S,)), dma((S,)),
            dma((T - 1,)), dma((T - 1,)), dma((T - 1,)), dma((T - 1,)),
        ],
        compiler_params=pltpu.CompilerParams(
            collective_id=0, has_side_effects=True, vmem_limit_bytes=52 * 1024 * 1024
        ),
    )(
        lengths, sibling_mask.reshape(-1), queries[0], keys[0], values[0],
        forward_out[0], logsumexp[0], up,
    )
    return dq[None], dk[None], dv[None]


def solution(mesh):
    placed = (
        P("thinker", "seq", None),
        P("thinker", "seq", None),
        P("thinker", "seq", None),
        P("thinker", "seq", None),
        P("thinker", None, "seq"),
        P(None, ("thinker", "seq"), None),
        P(),
        P("thinker", None, "seq"),
    )
    return jax.shard_map(
        shards,
        mesh=mesh,
        in_specs=placed,
        out_specs=(P("thinker", "seq", None), P("thinker", "seq", None), P("thinker", "seq", None)),
        check_vma=False,
    )
```

```python
import functools
import math

import jax
import jax.numpy as jnp
from jax import lax
from jax.experimental import pallas as pl
from jax.experimental.pallas import tpu as pltpu
from jax.sharding import PartitionSpec as P

BLOCK = 128
MESH = pl.DeviceIdType.MESH
F32 = jnp.float32
BF16 = jnp.bfloat16
FAR = 1e30


def dot_tt(a, b):
    return lax.dot_general(a, b, (((1,), (1,)), ((), ())), preferred_element_type=F32)


def dot_nn(a, b):
    return lax.dot_general(a, b, (((1,), (0,)), ((), ())), preferred_element_type=F32)


def dot_t(a, b):
    return lax.dot_general(a, b, (((0,), (0,)), ((), ())), preferred_element_type=F32)


def body(
    T, S, G, KV, HD,
    lengths, mask, q_ref, k_ref, v_ref, o_ref, lse_ref, up_ref,
    dq_ref, dk_ref, dv_ref,
    rows_in, kvall, sibc, sibp, gpart, gown, gsp, gspr, gsc, gz, gzr,
    qs, dos, lse2, delta, dqa, acc,
    up_send, up_recv, kv_send, kv_recv, z_send, z_recv, h_send, h_recv,
    g_send, g_recv, b_send, b_recv, y_send, y_recv,
):
    N = T * S
    ROWS = 128
    mid = T // 2
    W = up_ref.shape[1]
    C = (KV * G * HD) // W
    shift = int(math.log2(N))
    GQ = G * ROWS
    factor = HD ** (-0.5)
    log2e = math.log2(math.e)
    t = lax.axis_index("thinker")
    s = lax.axis_index("seq")
    me = t * S + s

    def place(d):
        return (d // S, d % S)

    barrier = pltpu.get_barrier_semaphore()

    def greet(i, c):
        pl.semaphore_signal(
            barrier, inc=1, device_id=place(lax.rem(me + i, N)), device_id_type=MESH
        )
        return c

    lax.fori_loop(1, N, greet, 0)

    for g in range(KV):
        kvall[s, g] = k_ref[:, g * HD:(g + 1) * HD]
        kvall[s, KV + g] = v_ref[:, g * HD:(g + 1) * HD]

    pl.semaphore_wait(barrier, N - 1)

    def remote(src, dst, ss, rs, where):
        return pltpu.make_async_remote_copy(
            src_ref=src, dst_ref=dst, send_sem=ss, recv_sem=rs,
            device_id=where, device_id_type=MESH,
        )

    def send_up(i, c):
        d = lax.rem(me + i, N)
        remote(
            up_ref.at[pl.ds(pl.multiple_of(d * 16, 16), 16)],
            rows_in.at[pl.ds(pl.multiple_of(me * 16, 16), 16)],
            up_send, up_recv, place(d),
        ).start()
        return c

    lax.fori_loop(1, N, send_up, 0)

    def z_copy(o):
        return remote(
            kvall.at[s], sibc.at[o - 1], z_send.at[o - 1], z_recv.at[o - 1],
            (lax.rem(t + T - o, T), s),
        )

    def near_in(o):
        return (t != 0) if o == 1 else (t != T - 1) if o == T - 1 else (t >= 0)

    order = (mid,) + tuple(o for o in range(1, T) if o != mid)
    for o in order:
        @pl.when(near_in(o))
        def _():
            z_copy(o).start()

    inner = (t == 1) | (t == T - 2)

    def z_pass():
        low = t == 1
        return remote(
            sibc.at[mid - 1], sibc.at[jnp.where(low, T - 2, 0)],
            z_send.at[T - 1], z_recv.at[jnp.where(low, T - 2, 0)],
            (jnp.where(low, 0, T - 1), s),
        )

    def kv_copy(d):
        return remote(kvall.at[s], kvall.at[s], kv_send.at[d], kv_recv.at[s], (t, d))

    def kv_start(d, c):
        kv_copy(d).start()
        return c

    lax.fori_loop(s + 1, S, kv_start, 0)

    rows_in[pl.ds(pl.multiple_of(me * 16, 16), 16), :] = up_ref[
        pl.ds(pl.multiple_of(me * 16, 16), 16), :
    ]
    mine = lengths[t]
    first = s * ROWS
    lane = lax.broadcasted_iota(jnp.int32, (1, GQ), 1) & (ROWS - 1)
    live = (first + lane) < mine
    for g in range(KV):
        qs[g] = jnp.concatenate(
            [q_ref[:, (g * G + i) * HD:(g * G + i + 1) * HD] for i in range(G)], axis=0
        )
        row = jnp.concatenate([lse_ref[g * G + i:g * G + i + 1, :] for i in range(G)], axis=1)
        lse2[g] = jnp.where(live, row * log2e, FAR)
    dqa[...] = jnp.zeros_like(dqa)

    @pl.when(s == 0)
    def _():
        sibp[...] = jnp.zeros_like(sibp)

    @pl.when(inner)
    def _():
        z_copy(mid).wait_recv()
        z_pass().start()

    whole = rows_in.at[pl.ds(0, (N - 1) * 16)]
    pltpu.make_async_copy(whole, whole, up_recv).wait()
    pos = lax.broadcasted_iota(jnp.int32, (ROWS, N * 16), 0)
    col = lax.broadcasted_iota(jnp.int32, (ROWS, N * 16), 1)
    base = (pos & (N - 1)) * 16 + lax.shift_right_logical(pos, shift) * C
    arrived = rows_in[...]
    per = W // HD
    for c in range(C):
        pick = jnp.where(col == base + c, 1.0, 0.0).astype(BF16)
        part = dot_nn(pick, arrived).astype(BF16)
        for i in range(per):
            h = c * per + i
            dos[h // G, (h % G) * ROWS:(h % G + 1) * ROWS, :] = part[:, i * HD:(i + 1) * HD]
    ones = jnp.ones((8, HD), BF16)
    for g in range(KV):
        og = jnp.concatenate(
            [o_ref[:, (g * G + i) * HD:(g * G + i + 1) * HD] for i in range(G)], axis=0
        )
        prod = dos[g].astype(F32) * og.astype(F32)
        high = prod.astype(BF16)
        low = (prod - high.astype(F32)).astype(BF16)
        delta[g] = (dot_tt(ones, high) + dot_tt(ones, low))[0:1, :]

    key_i = lax.broadcasted_iota(jnp.int32, (ROWS, GQ), 0)
    qry_i = lax.broadcasted_iota(jnp.int32, (ROWS, GQ), 1) & (ROWS - 1)
    scale = factor * log2e

    def own(b, diagonal):
        def step(g, c):
            km = kvall[b, g]
            vm = kvall[b, KV + g]
            qg = qs[g]
            dg = dos[g]
            p = jnp.exp2(dot_tt(km, qg) * scale - lse2[g])
            if diagonal:
                p = jnp.where(key_i <= qry_i, p, 0.0)
            ds = p * (dot_tt(vm, dg) - delta[g])
            pb = p.astype(BF16)
            db = ds.astype(BF16)
            dv = dot_nn(pb, dg)
            dk = dot_nn(db, qg) * factor
            if diagonal:
                acc[g] = dk
                acc[KV + g] = dv
            else:
                gpart[b, g] = dk.astype(BF16)
                gpart[b, KV + g] = dv.astype(BF16)
            dqa[g] += dot_t(db, km)
            return c

        lax.fori_loop(0, KV, step, 0)

    own(s, True)

    def shift_copy(o):
        return remote(
            sibc.at[o - 1], sibp.at[o - 1], h_send.at[o - 1], h_recv.at[o - 1],
            (t, lax.rem(s + 1, S)),
        )

    def back_copy(o):
        return remote(
            gsp.at[o - 1], gspr.at[o - 1], b_send.at[o - 1], b_recv.at[o - 1],
            (t, lax.rem(s + S - 1, S)),
        )

    for o in range(1, T):
        if o == mid:
            @pl.when(jnp.logical_not(inner))
            def _():
                z_copy(o).wait_recv()
        else:
            z_copy(o).wait_recv()

        @pl.when(s < S - 1)
        def _():
            shift_copy(o).start()

    for o in range(1, T):
        @pl.when(s > 0)
        def _():
            shift_copy(o).wait_recv()

        other = lengths[lax.rem(t + o, T)]
        edge = jnp.where(mask[o - 1] == 1, other - first, -2 * ROWS)

        def step(g, c):
            kc = sibc[o - 1, g]
            vc = sibc[o - 1, KV + g]
            kp = sibp[o - 1, g]
            vp = sibp[o - 1, KV + g]
            qg = qs[g]
            dg = dos[g]
            near = key_i <= qry_i
            place_k = jnp.where(near, key_i, key_i - ROWS)
            keep = (place_k < edge) & (place_k >= -first)
            st = jnp.where(near, dot_tt(kc, qg), dot_tt(kp, qg))
            p = jnp.where(keep, jnp.exp2(st * scale - lse2[g]), 0.0)
            dp = jnp.where(near, dot_tt(vc, dg), dot_tt(vp, dg))
            ds = p * (dp - delta[g])
            pc = jnp.where(near, p, 0.0).astype(BF16)
            pp = jnp.where(near, 0.0, p).astype(BF16)
            dc = jnp.where(near, ds, 0.0).astype(BF16)
            de = jnp.where(near, 0.0, ds).astype(BF16)
            gsc[o - 1, g] = dot_nn(dc, qg) * factor
            gsc[o - 1, KV + g] = dot_nn(pc, dg)
            gsp[o - 1, g] = (dot_nn(de, qg) * factor).astype(BF16)
            gsp[o - 1, KV + g] = dot_nn(pp, dg).astype(BF16)
            dqa[g] += dot_t(dc, kc) + dot_t(de, kp)
            return c

        lax.fori_loop(0, KV, step, 0)

        @pl.when(s > 0)
        def _():
            back_copy(o).start()

    def g_copy(b):
        return remote(gpart.at[b], gown.at[s], g_send.at[b], g_recv.at[s], (t, b))

    def kv_arrival(b):
        return remote(kvall.at[b], kvall.at[b], kv_send.at[b], kv_recv.at[b], (t, b))

    def own_step(b, c):
        kv_arrival(b).wait_recv()
        own(b, False)
        g_copy(b).start()
        return c

    half = s // 2
    lax.fori_loop(0, half, own_step, 0)

    def y_copy(o):
        return remote(
            gz.at[o - 1], gzr.at[o - 1], y_send.at[o - 1], y_recv.at[o - 1],
            (lax.rem(t + o, T), s),
        )

    for o in range(1, T):
        @pl.when(s < S - 1)
        def _():
            back_copy(o).wait_recv()
            gz[o - 1] = (gsc[o - 1] + gspr[o - 1].astype(F32)).astype(BF16)

        @pl.when(s == S - 1)
        def _():
            gz[o - 1] = gsc[o - 1].astype(BF16)

        y_copy(o).start()

    lax.fori_loop(half, s, own_step, 0)

    for g in range(KV):
        for i in range(G):
            h = g * G + i
            dq_ref[:, h * HD:(h + 1) * HD] = (
                dqa[g, i * ROWS:(i + 1) * ROWS, :] * factor
            ).astype(BF16)

    def g_arrival(b, c):
        remote(gpart.at[b], gown.at[b], g_send.at[b], g_recv.at[b], (t, b)).wait_recv()
        acc[...] += gown[b].astype(F32)
        return c

    lax.fori_loop(s + 1, S, g_arrival, 0)
    for o in range(1, T):
        y_copy(o).wait_recv()
        acc[...] += gzr[o - 1].astype(F32)
    for g in range(KV):
        dk_ref[:, g * HD:(g + 1) * HD] = acc[g].astype(BF16)
        dv_ref[:, g * HD:(g + 1) * HD] = acc[KV + g].astype(BF16)

    @pl.when(inner)
    def _():
        z_pass().wait_send()

    sent = up_ref.at[pl.ds(0, (N - 1) * 16)]
    pltpu.make_async_copy(sent, sent, up_send).wait()

    def kv_left(d, c):
        kv_copy(d).wait_send()
        return c

    lax.fori_loop(s + 1, S, kv_left, 0)

    def g_left(b, c):
        g_copy(b).wait_send()
        return c

    lax.fori_loop(0, s, g_left, 0)
    for o in range(1, T):
        @pl.when(near_in(o))
        def _():
            z_copy(o).wait_send()

        y_copy(o).wait_send()

        @pl.when(s < S - 1)
        def _():
            shift_copy(o).wait_send()

        @pl.when(s > 0)
        def _():
            back_copy(o).wait_send()


def shards(queries, keys, values, forward_out, logsumexp, upstream, lengths, sibling_mask):
    T = lax.axis_size("thinker")
    S = lax.axis_size("seq")
    N = T * S
    rows, qw = queries.shape[1:]
    kw = keys.shape[2]
    heads = logsumexp.shape[1]
    HD = qw // heads
    KV = kw // HD
    G = heads // KV
    width = (rows // N) * qw // 16
    up = upstream.reshape(N * 16, width)
    block = (2 * KV, rows, HD)
    vmem = pl.BlockSpec(memory_space=pltpu.VMEM)
    smem = pl.BlockSpec(memory_space=pltpu.SMEM)
    dma = pltpu.SemaphoreType.DMA
    dq, dk, dv = pl.pallas_call(
        functools.partial(body, T, S, G, KV, HD),
        out_shape=(
            jax.ShapeDtypeStruct((rows, qw), BF16),
            jax.ShapeDtypeStruct((rows, kw), BF16),
            jax.ShapeDtypeStruct((rows, kw), BF16),
        ),
        in_specs=[smem, smem] + [vmem] * 6,
        out_specs=(vmem, vmem, vmem),
        scratch_shapes=[
            pltpu.VMEM((N * 16, width), BF16),
            pltpu.VMEM((S,) + block, BF16),
            pltpu.VMEM((T - 1,) + block, BF16),
            pltpu.VMEM((T - 1,) + block, BF16),
            pltpu.VMEM((S,) + block, BF16),
            pltpu.VMEM((S,) + block, BF16),
            pltpu.VMEM((T - 1,) + block, BF16),
            pltpu.VMEM((T - 1,) + block, BF16),
            pltpu.VMEM((T - 1,) + block, F32),
            pltpu.VMEM((T - 1,) + block, BF16),
            pltpu.VMEM((T - 1,) + block, BF16),
            pltpu.VMEM((KV, G * rows, HD), BF16),
            pltpu.VMEM((KV, G * rows, HD), BF16),
            pltpu.VMEM((KV, 1, G * rows), F32),
            pltpu.VMEM((KV, 1, G * rows), F32),
            pltpu.VMEM((KV, G * rows, HD), F32),
            pltpu.VMEM(block, F32),
            dma, dma, dma((S,)), dma((S,)), dma((T,)), dma((T - 1,)),
            dma((T - 1,)), dma((T - 1,)), dma((S,)), dma((S,)),
            dma((T - 1,)), dma((T - 1,)), dma((T - 1,)), dma((T - 1,)),
        ],
        compiler_params=pltpu.CompilerParams(
            collective_id=0, has_side_effects=True, vmem_limit_bytes=52 * 1024 * 1024
        ),
    )(
        lengths, sibling_mask.reshape(-1), queries[0], keys[0], values[0],
        forward_out[0], logsumexp[0], up,
    )
    return dq[None], dk[None], dv[None]


def solution(mesh):
    placed = (
        P("thinker", "seq", None),
        P("thinker", "seq", None),
        P("thinker", "seq", None),
        P("thinker", "seq", None),
        P("thinker", None, "seq"),
        P(None, ("thinker", "seq"), None),
        P(),
        P("thinker", None, "seq"),
    )
    return jax.shard_map(
        shards,
        mesh=mesh,
        in_specs=placed,
        out_specs=(P("thinker", "seq", None), P("thinker", "seq", None), P("thinker", "seq", None)),
        check_vma=False,
    )
```

```python
import functools
import math

import jax
import jax.numpy as jnp
from jax import lax
from jax.experimental import pallas as pl
from jax.experimental.pallas import tpu as pltpu
from jax.sharding import PartitionSpec as P

BLOCK = 128
MESH = pl.DeviceIdType.MESH
F32 = jnp.float32
BF16 = jnp.bfloat16
FAR = 1e30


def dot_tt(a, b):
    return lax.dot_general(a, b, (((1,), (1,)), ((), ())), preferred_element_type=F32)


def dot_nn(a, b):
    return lax.dot_general(a, b, (((1,), (0,)), ((), ())), preferred_element_type=F32)


def dot_t(a, b):
    return lax.dot_general(a, b, (((0,), (0,)), ((), ())), preferred_element_type=F32)


def body(
    T, S, G, KV, HD,
    lengths, mask, q_ref, k_ref, v_ref, o_ref, lse_ref, up_ref,
    dq_ref, dk_ref, dv_ref,
    rows_in, kvall, sibc, sibp, gpart, gown, gsp, gspr, gsc, gz, gzr,
    qs, dos, lse2, delta, dqa, acc,
    up_send, up_recv, kv_send, kv_recv, z_send, z_recv, h_send, h_recv,
    g_send, g_recv, b_send, b_recv, y_send, y_recv,
):
    N = T * S
    ROWS = 128
    mid = T // 2
    W = up_ref.shape[1]
    C = (KV * G * HD) // W
    shift = int(math.log2(N))
    GQ = G * ROWS
    factor = HD ** (-0.5)
    log2e = math.log2(math.e)
    t = lax.axis_index("thinker")
    s = lax.axis_index("seq")
    me = t * S + s

    def place(d):
        return (d // S, d % S)

    barrier = pltpu.get_barrier_semaphore()

    def greet(i, c):
        pl.semaphore_signal(
            barrier, inc=1, device_id=place(lax.rem(me + i, N)), device_id_type=MESH
        )
        return c

    lax.fori_loop(1, N, greet, 0)

    for g in range(KV):
        kvall[s, g] = k_ref[:, g * HD:(g + 1) * HD]
        kvall[s, KV + g] = v_ref[:, g * HD:(g + 1) * HD]

    pl.semaphore_wait(barrier, N - 1)

    def remote(src, dst, ss, rs, where):
        return pltpu.make_async_remote_copy(
            src_ref=src, dst_ref=dst, send_sem=ss, recv_sem=rs,
            device_id=where, device_id_type=MESH,
        )

    def send_up(i, c):
        d = lax.rem(me + i, N)
        remote(
            up_ref.at[pl.ds(pl.multiple_of(d * 16, 16), 16)],
            rows_in.at[pl.ds(pl.multiple_of(me * 16, 16), 16)],
            up_send, up_recv, place(d),
        ).start()
        return c

    lax.fori_loop(1, N, send_up, 0)

    def z_copy(o):
        return remote(
            kvall.at[s], sibc.at[o - 1], z_send.at[o - 1], z_recv.at[o - 1],
            (lax.rem(t + T - o, T), s),
        )

    def near_in(o):
        return (t != 0) if o == 1 else (t != T - 1) if o == T - 1 else (t >= 0)

    order = (mid,) + tuple(o for o in range(1, T) if o != mid)
    for o in order:
        @pl.when(near_in(o))
        def _():
            z_copy(o).start()

    inner = (t == 1) | (t == T - 2)

    def z_pass():
        low = t == 1
        return remote(
            sibc.at[mid - 1], sibc.at[jnp.where(low, T - 2, 0)],
            z_send.at[T - 1], z_recv.at[jnp.where(low, T - 2, 0)],
            (jnp.where(low, 0, T - 1), s),
        )

    def kv_copy(d):
        return remote(kvall.at[s], kvall.at[s], kv_send.at[d], kv_recv.at[s], (t, d))

    def kv_start(d, c):
        kv_copy(d).start()
        return c

    lax.fori_loop(s + 1, S, kv_start, 0)

    rows_in[pl.ds(pl.multiple_of(me * 16, 16), 16), :] = up_ref[
        pl.ds(pl.multiple_of(me * 16, 16), 16), :
    ]
    mine = lengths[t]
    first = s * ROWS
    lane = lax.broadcasted_iota(jnp.int32, (1, GQ), 1) & (ROWS - 1)
    live = (first + lane) < mine
    for g in range(KV):
        qs[g] = jnp.concatenate(
            [q_ref[:, (g * G + i) * HD:(g * G + i + 1) * HD] for i in range(G)], axis=0
        )
        row = jnp.concatenate([lse_ref[g * G + i:g * G + i + 1, :] for i in range(G)], axis=1)
        lse2[g] = jnp.where(live, row * log2e, FAR)
    dqa[...] = jnp.zeros_like(dqa)

    @pl.when(s == 0)
    def _():
        sibp[...] = jnp.zeros_like(sibp)

    @pl.when(inner)
    def _():
        z_copy(mid).wait_recv()
        z_pass().start()

    whole = rows_in.at[pl.ds(0, (N - 1) * 16)]
    pltpu.make_async_copy(whole, whole, up_recv).wait()
    pos = lax.broadcasted_iota(jnp.int32, (ROWS, N * 16), 0)
    col = lax.broadcasted_iota(jnp.int32, (ROWS, N * 16), 1)
    base = (pos & (N - 1)) * 16 + lax.shift_right_logical(pos, shift) * C
    arrived = rows_in[...]
    per = W // HD
    for c in range(C):
        pick = jnp.where(col == base + c, 1.0, 0.0).astype(BF16)
        part = dot_nn(pick, arrived).astype(BF16)
        for i in range(per):
            h = c * per + i
            dos[h // G, (h % G) * ROWS:(h % G + 1) * ROWS, :] = part[:, i * HD:(i + 1) * HD]
    ones = jnp.ones((8, HD), BF16)
    for g in range(KV):
        og = jnp.concatenate(
            [o_ref[:, (g * G + i) * HD:(g * G + i + 1) * HD] for i in range(G)], axis=0
        )
        prod = dos[g].astype(F32) * og.astype(F32)
        high = prod.astype(BF16)
        low = (prod - high.astype(F32)).astype(BF16)
        delta[g] = (dot_tt(ones, high) + dot_tt(ones, low))[0:1, :]

    key_i = lax.broadcasted_iota(jnp.int32, (ROWS, GQ), 0)
    qry_i = lax.broadcasted_iota(jnp.int32, (ROWS, GQ), 1) & (ROWS - 1)
    scale = factor * log2e

    def own(b, diagonal):
        def step(g, c):
            km = kvall[b, g]
            vm = kvall[b, KV + g]
            qg = qs[g]
            dg = dos[g]
            p = jnp.exp2(dot_tt(km, qg) * scale - lse2[g])
            if diagonal:
                p = jnp.where(key_i <= qry_i, p, 0.0)
            ds = p * (dot_tt(vm, dg) - delta[g])
            pb = p.astype(BF16)
            db = ds.astype(BF16)
            dv = dot_nn(pb, dg)
            dk = dot_nn(db, qg) * factor
            if diagonal:
                acc[g] = dk
                acc[KV + g] = dv
            else:
                gpart[b, g] = dk.astype(BF16)
                gpart[b, KV + g] = dv.astype(BF16)
            dqa[g] += dot_t(db, km)
            return c

        lax.fori_loop(0, KV, step, 0)

    own(s, True)

    def shift_copy(o):
        return remote(
            sibc.at[o - 1], sibp.at[o - 1], h_send.at[o - 1], h_recv.at[o - 1],
            (t, lax.rem(s + 1, S)),
        )

    def back_copy(o):
        return remote(
            gsp.at[o - 1], gspr.at[o - 1], b_send.at[o - 1], b_recv.at[o - 1],
            (t, lax.rem(s + S - 1, S)),
        )

    for o in order:
        if o == mid:
            @pl.when(jnp.logical_not(inner))
            def _():
                z_copy(o).wait_recv()
        else:
            z_copy(o).wait_recv()

        @pl.when(s < S - 1)
        def _():
            shift_copy(o).start()

    for o in order:
        @pl.when(s > 0)
        def _():
            shift_copy(o).wait_recv()

        other = lengths[lax.rem(t + o, T)]
        edge = jnp.where(mask[o - 1] == 1, other - first, -2 * ROWS)

        def step(g, c):
            kc = sibc[o - 1, g]
            vc = sibc[o - 1, KV + g]
            kp = sibp[o - 1, g]
            vp = sibp[o - 1, KV + g]
            qg = qs[g]
            dg = dos[g]
            near = key_i <= qry_i
            place_k = jnp.where(near, key_i, key_i - ROWS)
            keep = (place_k < edge) & (place_k >= -first)
            st = jnp.where(near, dot_tt(kc, qg), dot_tt(kp, qg))
            p = jnp.where(keep, jnp.exp2(st * scale - lse2[g]), 0.0)
            dp = jnp.where(near, dot_tt(vc, dg), dot_tt(vp, dg))
            ds = p * (dp - delta[g])
            pc = jnp.where(near, p, 0.0).astype(BF16)
            pp = jnp.where(near, 0.0, p).astype(BF16)
            dc = jnp.where(near, ds, 0.0).astype(BF16)
            de = jnp.where(near, 0.0, ds).astype(BF16)
            gsc[o - 1, g] = dot_nn(dc, qg) * factor
            gsc[o - 1, KV + g] = dot_nn(pc, dg)
            gsp[o - 1, g] = (dot_nn(de, qg) * factor).astype(BF16)
            gsp[o - 1, KV + g] = dot_nn(pp, dg).astype(BF16)
            dqa[g] += dot_t(dc, kc) + dot_t(de, kp)
            return c

        lax.fori_loop(0, KV, step, 0)

        @pl.when(s > 0)
        def _():
            back_copy(o).start()

    def g_copy(b):
        return remote(gpart.at[b], gown.at[s], g_send.at[b], g_recv.at[s], (t, b))

    def kv_arrival(b):
        return remote(kvall.at[b], kvall.at[b], kv_send.at[b], kv_recv.at[b], (t, b))

    def own_step(b, c):
        kv_arrival(b).wait_recv()
        own(b, False)
        g_copy(b).start()
        return c

    half = s // 2
    lax.fori_loop(0, half, own_step, 0)

    def y_copy(o):
        return remote(
            gz.at[o - 1], gzr.at[o - 1], y_send.at[o - 1], y_recv.at[o - 1],
            (lax.rem(t + o, T), s),
        )

    for o in order:
        @pl.when(s < S - 1)
        def _():
            back_copy(o).wait_recv()
            gz[o - 1] = (gsc[o - 1] + gspr[o - 1].astype(F32)).astype(BF16)

        @pl.when(s == S - 1)
        def _():
            gz[o - 1] = gsc[o - 1].astype(BF16)

        y_copy(o).start()

    lax.fori_loop(half, s, own_step, 0)

    for g in range(KV):
        for i in range(G):
            h = g * G + i
            dq_ref[:, h * HD:(h + 1) * HD] = (
                dqa[g, i * ROWS:(i + 1) * ROWS, :] * factor
            ).astype(BF16)

    def g_arrival(b, c):
        remote(gpart.at[b], gown.at[b], g_send.at[b], g_recv.at[b], (t, b)).wait_recv()
        acc[...] += gown[b].astype(F32)
        return c

    lax.fori_loop(s + 1, S, g_arrival, 0)
    for o in range(1, T):
        y_copy(o).wait_recv()
        acc[...] += gzr[o - 1].astype(F32)
    for g in range(KV):
        dk_ref[:, g * HD:(g + 1) * HD] = acc[g].astype(BF16)
        dv_ref[:, g * HD:(g + 1) * HD] = acc[KV + g].astype(BF16)

    @pl.when(inner)
    def _():
        z_pass().wait_send()

    sent = up_ref.at[pl.ds(0, (N - 1) * 16)]
    pltpu.make_async_copy(sent, sent, up_send).wait()

    def kv_left(d, c):
        kv_copy(d).wait_send()
        return c

    lax.fori_loop(s + 1, S, kv_left, 0)

    def g_left(b, c):
        g_copy(b).wait_send()
        return c

    lax.fori_loop(0, s, g_left, 0)
    for o in range(1, T):
        @pl.when(near_in(o))
        def _():
            z_copy(o).wait_send()

        y_copy(o).wait_send()

        @pl.when(s < S - 1)
        def _():
            shift_copy(o).wait_send()

        @pl.when(s > 0)
        def _():
            back_copy(o).wait_send()


def shards(queries, keys, values, forward_out, logsumexp, upstream, lengths, sibling_mask):
    T = lax.axis_size("thinker")
    S = lax.axis_size("seq")
    N = T * S
    rows, qw = queries.shape[1:]
    kw = keys.shape[2]
    heads = logsumexp.shape[1]
    HD = qw // heads
    KV = kw // HD
    G = heads // KV
    width = (rows // N) * qw // 16
    up = upstream.reshape(N * 16, width)
    block = (2 * KV, rows, HD)
    vmem = pl.BlockSpec(memory_space=pltpu.VMEM)
    smem = pl.BlockSpec(memory_space=pltpu.SMEM)
    dma = pltpu.SemaphoreType.DMA
    dq, dk, dv = pl.pallas_call(
        functools.partial(body, T, S, G, KV, HD),
        out_shape=(
            jax.ShapeDtypeStruct((rows, qw), BF16),
            jax.ShapeDtypeStruct((rows, kw), BF16),
            jax.ShapeDtypeStruct((rows, kw), BF16),
        ),
        in_specs=[smem, smem] + [vmem] * 6,
        out_specs=(vmem, vmem, vmem),
        scratch_shapes=[
            pltpu.VMEM((N * 16, width), BF16),
            pltpu.VMEM((S,) + block, BF16),
            pltpu.VMEM((T - 1,) + block, BF16),
            pltpu.VMEM((T - 1,) + block, BF16),
            pltpu.VMEM((S,) + block, BF16),
            pltpu.VMEM((S,) + block, BF16),
            pltpu.VMEM((T - 1,) + block, BF16),
            pltpu.VMEM((T - 1,) + block, BF16),
            pltpu.VMEM((T - 1,) + block, F32),
            pltpu.VMEM((T - 1,) + block, BF16),
            pltpu.VMEM((T - 1,) + block, BF16),
            pltpu.VMEM((KV, G * rows, HD), BF16),
            pltpu.VMEM((KV, G * rows, HD), BF16),
            pltpu.VMEM((KV, 1, G * rows), F32),
            pltpu.VMEM((KV, 1, G * rows), F32),
            pltpu.VMEM((KV, G * rows, HD), F32),
            pltpu.VMEM(block, F32),
            dma, dma, dma((S,)), dma((S,)), dma((T,)), dma((T - 1,)),
            dma((T - 1,)), dma((T - 1,)), dma((S,)), dma((S,)),
            dma((T - 1,)), dma((T - 1,)), dma((T - 1,)), dma((T - 1,)),
        ],
        compiler_params=pltpu.CompilerParams(
            collective_id=0, has_side_effects=True, vmem_limit_bytes=52 * 1024 * 1024
        ),
    )(
        lengths, sibling_mask.reshape(-1), queries[0], keys[0], values[0],
        forward_out[0], logsumexp[0], up,
    )
    return dq[None], dk[None], dv[None]


def solution(mesh):
    placed = (
        P("thinker", "seq", None),
        P("thinker", "seq", None),
        P("thinker", "seq", None),
        P("thinker", "seq", None),
        P("thinker", None, "seq"),
        P(None, ("thinker", "seq"), None),
        P(),
        P("thinker", None, "seq"),
    )
    return jax.shard_map(
        shards,
        mesh=mesh,
        in_specs=placed,
        out_specs=(P("thinker", "seq", None), P("thinker", "seq", None), P("thinker", "seq", None)),
        check_vma=False,
    )
```

```python
import functools
import math

import jax
import jax.numpy as jnp
from jax import lax
from jax.experimental import pallas as pl
from jax.experimental.pallas import tpu as pltpu
from jax.sharding import PartitionSpec as P

BLOCK = 128
MESH = pl.DeviceIdType.MESH
F32 = jnp.float32
BF16 = jnp.bfloat16
FAR = 1e30


def dot_tt(a, b):
    return lax.dot_general(a, b, (((1,), (1,)), ((), ())), preferred_element_type=F32)


def dot_nn(a, b):
    return lax.dot_general(a, b, (((1,), (0,)), ((), ())), preferred_element_type=F32)


def dot_t(a, b):
    return lax.dot_general(a, b, (((0,), (0,)), ((), ())), preferred_element_type=F32)


def body(
    T, S, G, KV, HD,
    lengths, mask, q_ref, k_ref, v_ref, o_ref, lse_ref, up_ref,
    dq_ref, dk_ref, dv_ref,
    rows_in, kvall, sibc, sibp, gpart, gown, gsp, gspr, gsc, gz, gzr,
    qs, dos, lse2, delta, dqa, acc,
    up_send, up_recv, kv_send, kv_recv, z_send, z_recv, h_send, h_recv,
    g_send, g_recv, b_send, b_recv, y_send, y_recv,
):
    N = T * S
    ROWS = 128
    mid = T // 2
    W = up_ref.shape[1]
    C = (KV * G * HD) // W
    shift = int(math.log2(N))
    GQ = G * ROWS
    factor = HD ** (-0.5)
    log2e = math.log2(math.e)
    t = lax.axis_index("thinker")
    s = lax.axis_index("seq")
    me = t * S + s

    def place(d):
        return (d // S, d % S)

    barrier = pltpu.get_barrier_semaphore()

    def greet(i, c):
        pl.semaphore_signal(
            barrier, inc=1, device_id=place(lax.rem(me + i, N)), device_id_type=MESH
        )
        return c

    lax.fori_loop(1, N, greet, 0)

    for g in range(KV):
        kvall[s, g] = k_ref[:, g * HD:(g + 1) * HD]
        kvall[s, KV + g] = v_ref[:, g * HD:(g + 1) * HD]

    pl.semaphore_wait(barrier, N - 1)

    def remote(src, dst, ss, rs, where):
        return pltpu.make_async_remote_copy(
            src_ref=src, dst_ref=dst, send_sem=ss, recv_sem=rs,
            device_id=where, device_id_type=MESH,
        )

    def send_up(i, c):
        d = lax.rem(me + i, N)
        remote(
            up_ref.at[pl.ds(pl.multiple_of(d * 16, 16), 16)],
            rows_in.at[pl.ds(pl.multiple_of(me * 16, 16), 16)],
            up_send, up_recv, place(d),
        ).start()
        return c

    lax.fori_loop(1, N, send_up, 0)

    def z_copy(o):
        return remote(
            kvall.at[s], sibc.at[o - 1], z_send.at[o - 1], z_recv.at[o - 1],
            (lax.rem(t + T - o, T), s),
        )

    def near_in(o):
        return (t != 0) if o == 1 else (t != T - 1) if o == T - 1 else (t >= 0)

    order = (mid,) + tuple(o for o in range(1, T) if o != mid)
    for o in order:
        @pl.when(near_in(o))
        def _():
            z_copy(o).start()

    inner = (t == 1) | (t == T - 2)

    def z_pass():
        low = t == 1
        return remote(
            sibc.at[mid - 1], sibc.at[jnp.where(low, T - 2, 0)],
            z_send.at[T - 1], z_recv.at[jnp.where(low, T - 2, 0)],
            (jnp.where(low, 0, T - 1), s),
        )

    def kv_copy(d):
        return remote(kvall.at[s], kvall.at[s], kv_send.at[d], kv_recv.at[s], (t, d))

    def kv_start(d, c):
        kv_copy(d).start()
        return c

    lax.fori_loop(s + 1, S, kv_start, 0)

    rows_in[pl.ds(pl.multiple_of(me * 16, 16), 16), :] = up_ref[
        pl.ds(pl.multiple_of(me * 16, 16), 16), :
    ]
    mine = lengths[t]
    first = s * ROWS
    lane = lax.broadcasted_iota(jnp.int32, (1, GQ), 1) & (ROWS - 1)
    live = (first + lane) < mine
    for g in range(KV):
        qs[g] = jnp.concatenate(
            [q_ref[:, (g * G + i) * HD:(g * G + i + 1) * HD] for i in range(G)], axis=0
        )
        row = jnp.concatenate([lse_ref[g * G + i:g * G + i + 1, :] for i in range(G)], axis=1)
        lse2[g] = jnp.where(live, row * log2e, FAR)
    dqa[...] = jnp.zeros_like(dqa)

    @pl.when(s == 0)
    def _():
        sibp[...] = jnp.zeros_like(sibp)

    def shift_copy(o):
        return remote(
            sibc.at[o - 1], sibp.at[o - 1], h_send.at[o - 1], h_recv.at[o - 1],
            (t, lax.rem(s + 1, S)),
        )

    z_copy(mid).wait_recv()

    @pl.when(inner)
    def _():
        z_pass().start()

    @pl.when(s < S - 1)
    def _():
        shift_copy(mid).start()

    whole = rows_in.at[pl.ds(0, (N - 1) * 16)]
    pltpu.make_async_copy(whole, whole, up_recv).wait()
    pos = lax.broadcasted_iota(jnp.int32, (ROWS, N * 16), 0)
    col = lax.broadcasted_iota(jnp.int32, (ROWS, N * 16), 1)
    base = (pos & (N - 1)) * 16 + lax.shift_right_logical(pos, shift) * C
    arrived = rows_in[...]
    per = W // HD
    for c in range(C):
        pick = jnp.where(col == base + c, 1.0, 0.0).astype(BF16)
        part = dot_nn(pick, arrived).astype(BF16)
        for i in range(per):
            h = c * per + i
            dos[h // G, (h % G) * ROWS:(h % G + 1) * ROWS, :] = part[:, i * HD:(i + 1) * HD]
    ones = jnp.ones((8, HD), BF16)
    for g in range(KV):
        og = jnp.concatenate(
            [o_ref[:, (g * G + i) * HD:(g * G + i + 1) * HD] for i in range(G)], axis=0
        )
        prod = dos[g].astype(F32) * og.astype(F32)
        high = prod.astype(BF16)
        low = (prod - high.astype(F32)).astype(BF16)
        delta[g] = (dot_tt(ones, high) + dot_tt(ones, low))[0:1, :]

    key_i = lax.broadcasted_iota(jnp.int32, (ROWS, GQ), 0)
    qry_i = lax.broadcasted_iota(jnp.int32, (ROWS, GQ), 1) & (ROWS - 1)
    scale = factor * log2e

    def own(b, diagonal):
        def step(g, c):
            km = kvall[b, g]
            vm = kvall[b, KV + g]
            qg = qs[g]
            dg = dos[g]
            p = jnp.exp2(dot_tt(km, qg) * scale - lse2[g])
            if diagonal:
                p = jnp.where(key_i <= qry_i, p, 0.0)
            ds = p * (dot_tt(vm, dg) - delta[g])
            pb = p.astype(BF16)
            db = ds.astype(BF16)
            dv = dot_nn(pb, dg)
            dk = dot_nn(db, qg) * factor
            if diagonal:
                acc[g] = dk
                acc[KV + g] = dv
            else:
                gpart[b, g] = dk.astype(BF16)
                gpart[b, KV + g] = dv.astype(BF16)
            dqa[g] += dot_t(db, km)
            return c

        lax.fori_loop(0, KV, step, 0)

    def back_copy(o):
        return remote(
            gsp.at[o - 1], gspr.at[o - 1], b_send.at[o - 1], b_recv.at[o - 1],
            (t, lax.rem(s + S - 1, S)),
        )

    for o in order[1:]:
        z_copy(o).wait_recv()

        @pl.when(s < S - 1)
        def _():
            shift_copy(o).start()

    for o in order:
        @pl.when(s > 0)
        def _():
            shift_copy(o).wait_recv()

        other = lengths[lax.rem(t + o, T)]
        edge = jnp.where(mask[o - 1] == 1, other - first, -2 * ROWS)

        def step(g, c):
            kc = sibc[o - 1, g]
            vc = sibc[o - 1, KV + g]
            kp = sibp[o - 1, g]
            vp = sibp[o - 1, KV + g]
            qg = qs[g]
            dg = dos[g]
            near = key_i <= qry_i
            place_k = jnp.where(near, key_i, key_i - ROWS)
            keep = (place_k < edge) & (place_k >= -first)
            st = jnp.where(near, dot_tt(kc, qg), dot_tt(kp, qg))
            p = jnp.where(keep, jnp.exp2(st * scale - lse2[g]), 0.0)
            dp = jnp.where(near, dot_tt(vc, dg), dot_tt(vp, dg))
            ds = p * (dp - delta[g])
            pc = jnp.where(near, p, 0.0).astype(BF16)
            pp = jnp.where(near, 0.0, p).astype(BF16)
            dc = jnp.where(near, ds, 0.0).astype(BF16)
            de = jnp.where(near, 0.0, ds).astype(BF16)
            gsc[o - 1, g] = dot_nn(dc, qg) * factor
            gsc[o - 1, KV + g] = dot_nn(pc, dg)
            gsp[o - 1, g] = (dot_nn(de, qg) * factor).astype(BF16)
            gsp[o - 1, KV + g] = dot_nn(pp, dg).astype(BF16)
            dqa[g] += dot_t(dc, kc) + dot_t(de, kp)
            return c

        lax.fori_loop(0, KV, step, 0)

        @pl.when(s > 0)
        def _():
            back_copy(o).start()

    def g_copy(b):
        return remote(gpart.at[b], gown.at[s], g_send.at[b], g_recv.at[s], (t, b))

    def kv_arrival(b):
        return remote(kvall.at[b], kvall.at[b], kv_send.at[b], kv_recv.at[b], (t, b))

    def own_step(b, c):
        kv_arrival(b).wait_recv()
        own(b, False)
        g_copy(b).start()
        return c

    own(s, True)
    half = s // 2
    lax.fori_loop(0, half, own_step, 0)

    def y_copy(o):
        return remote(
            gz.at[o - 1], gzr.at[o - 1], y_send.at[o - 1], y_recv.at[o - 1],
            (lax.rem(t + o, T), s),
        )

    for o in order:
        @pl.when(s < S - 1)
        def _():
            back_copy(o).wait_recv()
            gz[o - 1] = (gsc[o - 1] + gspr[o - 1].astype(F32)).astype(BF16)

        @pl.when(s == S - 1)
        def _():
            gz[o - 1] = gsc[o - 1].astype(BF16)

        y_copy(o).start()

    lax.fori_loop(half, s, own_step, 0)

    for g in range(KV):
        for i in range(G):
            h = g * G + i
            dq_ref[:, h * HD:(h + 1) * HD] = (
                dqa[g, i * ROWS:(i + 1) * ROWS, :] * factor
            ).astype(BF16)

    def g_arrival(b, c):
        remote(gpart.at[b], gown.at[b], g_send.at[b], g_recv.at[b], (t, b)).wait_recv()
        acc[...] += gown[b].astype(F32)
        return c

    lax.fori_loop(s + 1, S, g_arrival, 0)
    for o in range(1, T):
        y_copy(o).wait_recv()
        acc[...] += gzr[o - 1].astype(F32)
    for g in range(KV):
        dk_ref[:, g * HD:(g + 1) * HD] = acc[g].astype(BF16)
        dv_ref[:, g * HD:(g + 1) * HD] = acc[KV + g].astype(BF16)

    @pl.when(inner)
    def _():
        z_pass().wait_send()

    sent = up_ref.at[pl.ds(0, (N - 1) * 16)]
    pltpu.make_async_copy(sent, sent, up_send).wait()

    def kv_left(d, c):
        kv_copy(d).wait_send()
        return c

    lax.fori_loop(s + 1, S, kv_left, 0)

    def g_left(b, c):
        g_copy(b).wait_send()
        return c

    lax.fori_loop(0, s, g_left, 0)
    for o in range(1, T):
        @pl.when(near_in(o))
        def _():
            z_copy(o).wait_send()

        y_copy(o).wait_send()

        @pl.when(s < S - 1)
        def _():
            shift_copy(o).wait_send()

        @pl.when(s > 0)
        def _():
            back_copy(o).wait_send()


def shards(queries, keys, values, forward_out, logsumexp, upstream, lengths, sibling_mask):
    T = lax.axis_size("thinker")
    S = lax.axis_size("seq")
    N = T * S
    rows, qw = queries.shape[1:]
    kw = keys.shape[2]
    heads = logsumexp.shape[1]
    HD = qw // heads
    KV = kw // HD
    G = heads // KV
    width = (rows // N) * qw // 16
    up = upstream.reshape(N * 16, width)
    block = (2 * KV, rows, HD)
    vmem = pl.BlockSpec(memory_space=pltpu.VMEM)
    smem = pl.BlockSpec(memory_space=pltpu.SMEM)
    dma = pltpu.SemaphoreType.DMA
    dq, dk, dv = pl.pallas_call(
        functools.partial(body, T, S, G, KV, HD),
        out_shape=(
            jax.ShapeDtypeStruct((rows, qw), BF16),
            jax.ShapeDtypeStruct((rows, kw), BF16),
            jax.ShapeDtypeStruct((rows, kw), BF16),
        ),
        in_specs=[smem, smem] + [vmem] * 6,
        out_specs=(vmem, vmem, vmem),
        scratch_shapes=[
            pltpu.VMEM((N * 16, width), BF16),
            pltpu.VMEM((S,) + block, BF16),
            pltpu.VMEM((T - 1,) + block, BF16),
            pltpu.VMEM((T - 1,) + block, BF16),
            pltpu.VMEM((S,) + block, BF16),
            pltpu.VMEM((S,) + block, BF16),
            pltpu.VMEM((T - 1,) + block, BF16),
            pltpu.VMEM((T - 1,) + block, BF16),
            pltpu.VMEM((T - 1,) + block, F32),
            pltpu.VMEM((T - 1,) + block, BF16),
            pltpu.VMEM((T - 1,) + block, BF16),
            pltpu.VMEM((KV, G * rows, HD), BF16),
            pltpu.VMEM((KV, G * rows, HD), BF16),
            pltpu.VMEM((KV, 1, G * rows), F32),
            pltpu.VMEM((KV, 1, G * rows), F32),
            pltpu.VMEM((KV, G * rows, HD), F32),
            pltpu.VMEM(block, F32),
            dma, dma, dma((S,)), dma((S,)), dma((T,)), dma((T - 1,)),
            dma((T - 1,)), dma((T - 1,)), dma((S,)), dma((S,)),
            dma((T - 1,)), dma((T - 1,)), dma((T - 1,)), dma((T - 1,)),
        ],
        compiler_params=pltpu.CompilerParams(
            collective_id=0, has_side_effects=True, vmem_limit_bytes=52 * 1024 * 1024
        ),
    )(
        lengths, sibling_mask.reshape(-1), queries[0], keys[0], values[0],
        forward_out[0], logsumexp[0], up,
    )
    return dq[None], dk[None], dv[None]


def solution(mesh):
    placed = (
        P("thinker", "seq", None),
        P("thinker", "seq", None),
        P("thinker", "seq", None),
        P("thinker", "seq", None),
        P("thinker", None, "seq"),
        P(None, ("thinker", "seq"), None),
        P(),
        P("thinker", None, "seq"),
    )
    return jax.shard_map(
        shards,
        mesh=mesh,
        in_specs=placed,
        out_specs=(P("thinker", "seq", None), P("thinker", "seq", None), P("thinker", "seq", None)),
        check_vma=False,
    )
```
